32 devices in a mesh: row: 4 (over z), col: 8 (over y, x, core).
Axes of the slice: x: 2, y: 2, z: 4, core: 2. Of those that a mesh axis runs over, the one named last changes fastest.
Arguments:
- student: bfloat16 [4096, 2048], P(('row', 'col')), may hold values from -6 to 6
- codes: bfloat16 [4096, 3584], P(('row', 'col')), may hold values from -6 to 6
- scales: bfloat16 [4096, 28], P(('row', 'col')), may hold values from 0.25 to 4
- slot: int32 [4096], P(('row', 'col')), may hold values from 0 to 511, as said below
Outputs:
- loss: float32 [], replicated
- student_grad: float32 [4096, 2048], P(('row', 'col'))
The draws below stay inside these ranges and needn't reach their ends.
Inputs may be any that keep to these rules, and one draw needn't show every extreme that they name: For the teacher rows held by the devices of one col index, slot lists each of 0 to 511 exactly once.
All inputs are finite; a program needn't handle non-finite values.
Results may differ from the reference program's by a relative error of at most 0.0048.
The reference program's roundings to bfloat16 on the way count: a program that leaves them out, or rounds other values in their place, can miss the bound.
Values may be sent and summed in bfloat16 or wider, within the bound.
A program may use at most 128 MiB of HBM per device.

```python
import math
import jax
import jax.numpy as jnp
from jax import lax

DS = 2048
DT = 3584
GROUP = 128
R_DEV = 128
CBLK = 512
BATCH = 4096
N_COL = 8


def draw_slot(key, part):
    key = jax.random.fold_in(key, 7)
    columns = BATCH // CBLK
    row_count = CBLK // R_DEV
    keys = jax.random.split(key, columns)
    orders = jax.vmap(lambda single: jax.random.permutation(single, CBLK))(keys)
    return orders.reshape(columns, row_count, R_DEV).transpose(1, 0, 2).reshape(BATCH).astype(jnp.int32)


def shard_levels(rng, dims, shards, least, largest):
    factor_of, own = 1.0, jax.random.fold_in(rng, 6)
    for axis_at, blocks in shards:
        draws = jnp.exp(jax.random.uniform(jax.random.fold_in(own, axis_at), (blocks,), jnp.float32, least / len(shards), largest / len(shards)))
        factor_of = factor_of * jnp.repeat(draws, dims[axis_at] // blocks).reshape([-1 if axis == axis_at else 1 for axis in range(len(dims))])
    return factor_of


def centred(rng, dims, scale, bound, cuts=(), held_as=jnp.bfloat16):
    drawn = jax.random.normal(rng, dims, jnp.float32) * scale
    if len(cuts) > 0:
        drawn = shard_levels(rng, dims, cuts, -0.22, 0.18) * drawn
    return jnp.clip(drawn, min=-bound, max=bound).astype(held_as)


def setup_inputs(seed: int = 0) -> dict:
    key_list = jax.random.split(jax.random.key(seed), 5)
    student = centred(key_list[0], (BATCH, DS), 1.0, 6.0, ((0, 32),))
    codes = centred(key_list[1], (BATCH, DT), 1.0, 6.0, ((0, 32),))
    scales = jnp.clip(jnp.exp(math.log(4.0) - 2.7725887 * jax.random.uniform(key_list[2], (BATCH, DT // GROUP), jnp.float32) ** shard_levels(key_list[2], (BATCH, DT // GROUP), ((0, 32),), -0.2, 0.2)), 0.25, 4.0).astype(jnp.bfloat16)
    slot = draw_slot(jax.random.fold_in(key_list[4], 71), 0)
    return dict(student=student, codes=codes, scales=scales, slot=slot)


def unit_rows(values):
    inverse_norm = lax.rsqrt(lax.optimization_barrier(jnp.sum(values * values, axis=1, keepdims=True)) + 1e-06)
    return (values * inverse_norm, inverse_norm)

def dequantize(codes, scales):
    rows = codes.shape[0]
    grouped = codes.astype(jnp.float32).reshape(rows, scales.shape[1], -1) * scales.astype(jnp.float32)[:, :, None]
    return grouped.reshape(rows, -1)

def reference(student, codes, scales, slot):
    unit, inverse_norm = unit_rows(student.astype(jnp.float32))
    student_unit = unit.astype(jnp.bfloat16)
    teacher_server = unit_rows(dequantize(codes, scales))[0].astype(jnp.bfloat16)
    position = jnp.arange(BATCH, dtype=jnp.int32)
    column = position // R_DEV % N_COL
    target = (slot // R_DEV * N_COL + column) * R_DEV + slot % R_DEV
    teacher_unit = jnp.zeros((BATCH, DT), jnp.bfloat16).at[target].set(teacher_server)
    block_rows = min(512, BATCH)

    def per_block(start):
        student_block = lax.dynamic_slice_in_dim(student_unit, start, block_rows, 0)
        teacher_block = lax.dynamic_slice_in_dim(teacher_unit, start, block_rows, 0)
        gram_student = jnp.dot(student_block, student_unit.T, preferred_element_type=jnp.float32)
        gram_teacher = jnp.dot(teacher_block, teacher_unit.T, preferred_element_type=jnp.float32)
        differ = gram_student - gram_teacher
        rounded = differ.astype(jnp.bfloat16)
        grad_block = DS * jnp.dot(rounded, student_unit, preferred_element_type=jnp.float32)
        return (jnp.sum(differ * differ), grad_block)
    starts = jnp.arange(BATCH // block_rows, dtype=jnp.int32) * block_rows
    partial_sums, grad_blocks = lax.map(per_block, starts)
    loss = jnp.sum(partial_sums) * (DS / (BATCH * BATCH))
    grad_unit = grad_blocks.reshape(BATCH, DS)
    along = lax.optimization_barrier(jnp.sum(unit * grad_unit, axis=1, keepdims=True))
    student_grad = inverse_norm * (grad_unit - unit * along)
    return (loss, student_grad)
```

```python
import functools

import jax
import jax.numpy as jnp
from jax import lax
from jax.experimental import pallas as pl
from jax.experimental.pallas import tpu as pltpu
from jax.sharding import PartitionSpec as P

MESH = pl.DeviceIdType.MESH
F32 = jnp.float32
BF16 = jnp.bfloat16


def flip(index, bit):
    return index + bit * (1 - 2 * ((index // bit) % 2))


def flip_all(index, mask):
    bit = 1
    while bit <= mask:
        if mask & bit:
            index = flip(index, bit)
        bit *= 2
    return index


def kernel(
    rows_n, cols_n, total_rows, student, codes, scales, slot, loss_out, grad_out,
    s_row, s_col, t_raw, t_col, t_row, places, slots, core_got, got, total,
    loss_z, loss_put, loss_got, loss_sum, send, recv,
):
    r = student.shape[0]
    ds = student.shape[1]
    dt = codes.shape[1]
    group = dt // scales.shape[1]
    a = lax.axis_index("row")
    c = lax.axis_index("col")
    chips = cols_n // 2
    bits = []
    bit = cols_n // 2
    while bit > 1:
        bits.append(bit)
        bit //= 2
    orders = (tuple(bits), tuple(reversed(bits)))
    core = c % 2
    chip = c // 2
    counter = [0]

    def take(count=1):
        counter[0] += count
        return counter[0] - count

    def copy_to(src, dst, index, device):
        return pltpu.make_async_remote_copy(
            src_ref=src, dst_ref=dst, send_sem=send.at[index], recv_sem=recv.at[index],
            device_id=device, device_id_type=MESH,
        )

    def block(index, size=r):
        return pl.ds(pl.multiple_of(index * size, size), size)

    barrier = pltpu.get_barrier_semaphore()
    for k in range(1, rows_n):
        pl.semaphore_signal(barrier, inc=1, device_id=((a + k) % rows_n, c), device_id_type=MESH)
    for bit in bits + [1]:
        pl.semaphore_signal(barrier, inc=1, device_id=(a, flip(c, bit)), device_id_type=MESH)

    squares = jnp.zeros((r, group), F32)
    for g in range(dt // group):
        part = codes[:, g * group:(g + 1) * group].astype(F32) * scales[:, g:g + 1].astype(F32)
        squares = squares + part * part
    inverse = lax.rsqrt(jnp.sum(squares, axis=1, keepdims=True) + 1e-06)
    for g in range(dt // group):
        part = codes[:, g * group:(g + 1) * group].astype(F32) * scales[:, g:g + 1].astype(F32)
        t_raw[block(a), g * group:(g + 1) * group] = (part * inverse).astype(BF16)
    slots[a] = jnp.broadcast_to(slot[...], slots.shape[1:])

    pl.semaphore_wait(barrier, rows_n - 1 + len(bits) + 1)

    def line(refs):
        base = take(len(refs) * 2 * (rows_n - 1))

        def each(step, up, act):
            for n, (ref, view) in enumerate(refs):
                index = base + (n * 2 + up) * (rows_n - 1) + step
                act(ref, view, index)

        def start(step):
            for up in (1, 0):
                held = a - step if up else a + step
                ok = (held >= 0) & (a < rows_n - 1) if up else (held < rows_n) & (a > 0)
                to = (a + 1 if up else a - 1, c)

                @pl.when(ok)
                def _():
                    each(step, up, lambda ref, view, index: copy_to(
                        view(ref, held), view(ref, held), index, to).start())

        def wait_recv(step):
            for up in (1, 0):
                held = a - 1 - step if up else a + 1 + step
                ok = held >= 0 if up else held < rows_n

                @pl.when(ok)
                def _():
                    each(step, up, lambda ref, view, index: copy_to(
                        view(ref, held), view(ref, held), index, (a, c)).wait_recv())

        def wait_send():
            for step in range(rows_n - 1):
                for up in (1, 0):
                    held = a - step if up else a + step
                    ok = (held >= 0) & (a < rows_n - 1) if up else (held < rows_n) & (a > 0)

                    @pl.when(ok)
                    def _():
                        each(step, up, lambda ref, view, index: copy_to(
                            view(ref, held), view(ref, held), index, (a, c)).wait_send())

        return start, wait_recv, wait_send

    def plane(ref, width):
        half = width // 2
        started = []
        steps = len(bits)
        pending = {}

        def start(step):
            todo = []
            for h in (0, 1):
                order = orders[h]
                masks = [0]
                for bit in order[:step]:
                    masks = masks + [mask + bit for mask in masks]
                for mask in masks:
                    index = take()
                    view = ref.at[block(flip_all(c, mask)), h * half:(h + 1) * half]
                    copy = copy_to(view, view, index, (a, flip(c, order[step])))
                    copy.start()
                    started.append(copy)
                    todo.append(copy)
            pending[step] = todo

        def start_core():
            todo = []
            for mask in range(0, cols_n, 2):
                index = take()
                view = ref.at[block(flip_all(c, mask)), 0:width]
                copy = copy_to(view, view, index, (a, flip(c, 1)))
                copy.start()
                started.append(copy)
                todo.append(copy)
            pending[steps] = todo

        def wait_recv(step):
            for copy in pending[step]:
                copy.wait_recv()

        def wait_send():
            for copy in started:
                copy.wait_send()

        return start, start_core, wait_recv, wait_send

    whole = lambda ref, held: ref.at[block(held)]
    page = lambda ref, held: ref.at[held]
    t_start, t_recv, t_sent = line([(t_raw, whole), (slots, page)])
    t_start(0)

    values = student[...].astype(F32)
    inverse_norm = lax.rsqrt(jnp.sum(values * values, axis=1, keepdims=True) + 1e-06)
    unit = (values * inverse_norm).astype(BF16)
    s_row[block(c)] = unit
    s_col[block(a)] = unit

    steps = len(bits)
    p_start, p_core, p_recv, p_sent = plane(s_row, ds)
    p_start(0)
    p_recv(0)
    for step in range(1, steps):
        p_start(step)
        p_recv(step)
    p_core()
    for step in range(rows_n - 1):
        t_recv(step)
        if step + 1 < rows_n - 1:
            t_start(step + 1)

    s_start, s_recv, s_sent = line([(s_col, whole)])
    s_start(0)

    column = rows_n * r
    for b in range(rows_n):
        at = lax.broadcasted_iota(jnp.int32, (column, r), 0)
        places[:, b * r:(b + 1) * r] = (at == slots[b][0:1, :]).astype(F32).astype(BF16)
    piece = 512

    def own(n, carry):
        cut = block(n, piece)
        t_row[block(c), cut] = jnp.dot(
            places[block(a), :], t_raw[:, cut], preferred_element_type=F32).astype(BF16)
        return carry

    lax.fori_loop(0, dt // piece, own, 0)
    q_start, q_core, q_recv, q_sent = plane(t_row, dt)
    q_start(0)

    def every(n, carry):
        cut = block(n, piece)
        t_col[:, cut] = jnp.dot(places[...], t_raw[:, cut], preferred_element_type=F32).astype(BF16)
        return carry

    lax.fori_loop(0, dt // piece, every, 0)
    q_recv(0)
    for step in range(1, steps):
        q_start(step)
        if step <= rows_n - 2:
            s_recv(step - 1)
            s_start(step)
        q_recv(step)
    q_core()
    for step in range(min(steps, rows_n - 1) - 1, rows_n - 1):
        s_recv(step)
        if step + 1 < rows_n - 1:
            s_start(step + 1)
    p_recv(steps)
    q_recv(steps)
    q_sent()

    loss_sum[...] = jnp.zeros_like(loss_sum)
    core_base = take(chips)
    contract = (((1,), (1,)), ((), ()))

    def core_copy(i, there):
        return copy_to(
            t_row.at[block(there * 2 + 1 - core), 0:ds], core_got.at[i], core_base + i, (a, flip(c, 1)))

    def tile(i, carry):
        there = (chip + 1 + i) % chips
        pair = block(there, 2 * r)
        differ = lax.dot_general(s_row[pair, :], s_col[...], contract, preferred_element_type=F32)
        differ = differ - lax.dot_general(t_row[pair, :], t_col[...], contract, preferred_element_type=F32)
        loss_sum[...] += jnp.sum(differ * differ, axis=0, keepdims=True)
        low = differ.astype(BF16)
        for n in range(ds // piece):
            t_row[pair, n * piece:(n + 1) * piece] = jnp.dot(
                low, s_col[:, n * piece:(n + 1) * piece], preferred_element_type=F32).astype(BF16)
        core_copy(i, there).start()
        return carry

    lax.fori_loop(0, chips, tile, 0)

    loss_z[a] = jnp.broadcast_to(jnp.sum(loss_sum[...], axis=1, keepdims=True), loss_z.shape[1:])
    loss_copies = []
    for k in range(1, rows_n):
        copy = copy_to(loss_z.at[a], loss_z.at[a], take(), ((a + k) % rows_n, c))
        copy.start()
        loss_copies.append(copy)

    def join(i, carry):
        there = (chip + 1 + i) % chips
        core_copy(i, there).wait_recv()
        mine = block(there * 2 + core)
        t_row[mine, 0:ds] = (t_row[mine, 0:ds].astype(F32) + core_got[i].astype(F32)).astype(BF16)
        return carry

    lax.fori_loop(0, chips - 1, join, 0)
    core_copy(chips - 1, chip).wait_recv()
    total[...] = t_row[block(c), 0:ds].astype(F32) + core_got[chips - 1].astype(F32)

    half = ds // 2
    left = [list(range(0, cols_n, 2)) for _ in (0, 1)]
    sent = []
    got_at = 0
    for k, copy in enumerate(loss_copies):
        copy.wait_recv()
    loss_now = loss_z[0]
    for b in range(1, rows_n):
        loss_now = loss_now + loss_z[b]
    loss_bits = bits + [1]
    for step in range(steps):
        todo = []
        loss_put[step] = loss_now
        loss_copy = copy_to(loss_put.at[step], loss_got.at[step], take(), (a, flip(c, loss_bits[step])))
        loss_copy.start()
        for h in (0, 1):
            bit = tuple(reversed(orders[h]))[step]
            keep = [mask for mask in left[h] if not mask & bit]
            for mask in keep:
                away = t_row.at[block(flip_all(c, mask + bit)), h * half:(h + 1) * half]
                copy = copy_to(away, got.at[got_at], take(), (a, flip(c, bit)))
                copy.start()
                todo.append((h, mask, copy, got_at))
                got_at += 1
            left[h] = keep
        loss_copy.wait_recv()
        loss_now = loss_now + loss_got[step]
        sent.append(loss_copy)
        for h, mask, copy, index in todo:
            copy.wait_recv()
            sent.append(copy)
            span = slice(h * half, (h + 1) * half)
            if mask == 0:
                total[:, span] += got[index].astype(F32)
            else:
                mine = block(flip_all(c, mask))
                t_row[mine, span] = (t_row[mine, span].astype(F32) + got[index].astype(F32)).astype(BF16)
    loss_put[steps] = loss_now
    copy = copy_to(loss_put.at[steps], loss_got.at[steps], take(), (a, flip(c, 1)))
    copy.start()
    sent.append(copy)

    grad = total[...] * float(ds)
    values = student[...].astype(F32)
    inverse_norm = lax.rsqrt(jnp.sum(values * values, axis=1, keepdims=True) + 1e-06)
    unit = values * inverse_norm
    along = jnp.sum(unit * grad, axis=1, keepdims=True)
    grad_out[...] = inverse_norm * (grad - unit * along)

    copy.wait_recv()
    loss_out[...] = (loss_now + loss_got[steps]) * (ds / (total_rows * total_rows))

    for copy in sent + loss_copies:
        copy.wait_send()
    for i in range(chips):
        core_copy(i, (chip + 1 + i) % chips).wait_send()
    t_sent()
    s_sent()
    p_sent()


def on_device(rows_n, cols_n, student, codes, scales, slot):
    r, ds = student.shape
    dt = codes.shape[1]
    total_rows = r * rows_n * cols_n
    chips = cols_n // 2
    steps = chips.bit_length() - 1
    count = 6 * (rows_n - 1) + 2 * (2 * (chips - 1) + chips)
    count += chips + (rows_n - 1) + 2 * (chips - 1) + steps + 1
    vmem = pl.BlockSpec(memory_space=pltpu.VMEM)
    loss, grad = pl.pallas_call(
        functools.partial(kernel, rows_n, cols_n, total_rows),
        out_shape=(jax.ShapeDtypeStruct((8, 128), F32), jax.ShapeDtypeStruct((r, ds), F32)),
        in_specs=[vmem] * 4,
        out_specs=(vmem, vmem),
        scratch_shapes=[
            pltpu.VMEM((cols_n * r, ds), BF16),
            pltpu.VMEM((rows_n * r, ds), BF16),
            pltpu.VMEM((rows_n * r, dt), BF16),
            pltpu.VMEM((rows_n * r, dt), BF16),
            pltpu.VMEM((cols_n * r, dt), BF16),
            pltpu.VMEM((rows_n * r, rows_n * r), BF16),
            pltpu.VMEM((rows_n, 8, r), jnp.int32),
            pltpu.VMEM((chips, r, ds), BF16),
            pltpu.VMEM((2 * (chips - 1), r, ds // 2), BF16),
            pltpu.VMEM((r, ds), F32),
            pltpu.VMEM((rows_n, 8, 128), F32),
            pltpu.VMEM((steps + 1, 8, 128), F32),
            pltpu.VMEM((steps + 1, 8, 128), F32),
            pltpu.VMEM((1, rows_n * r), F32),
            pltpu.SemaphoreType.DMA((count,)),
            pltpu.SemaphoreType.DMA((count,)),
        ],
        compiler_params=pltpu.CompilerParams(
            collective_id=0, has_side_effects=True, vmem_limit_bytes=62 * 1024 * 1024
        ),
    )(student, codes, scales, slot.reshape(1, r))
    return loss[0, 0], grad


def solution(mesh):
    rows_n, cols_n = mesh.shape["row"], mesh.shape["col"]
    return jax.shard_map(
        functools.partial(on_device, rows_n, cols_n),
        mesh=mesh,
        in_specs=(
            P(("row", "col"), None),
            P(("row", "col"), None),
            P(("row", "col"), None),
            P(("row", "col")),
        ),
        out_specs=(P(), P(("row", "col"), None)),
        check_vma=False,
    )
```

```python
import functools

import jax
import jax.numpy as jnp
from jax import lax
from jax.experimental import pallas as pl
from jax.experimental.pallas import tpu as pltpu
from jax.sharding import PartitionSpec as P

MESH = pl.DeviceIdType.MESH
F32 = jnp.float32
BF16 = jnp.bfloat16


def flip(index, bit):
    return index + bit * (1 - 2 * ((index // bit) % 2))


def flip_all(index, mask):
    bit = 1
    while bit <= mask:
        if mask & bit:
            index = flip(index, bit)
        bit *= 2
    return index


def kernel(
    rows_n, cols_n, total_rows, student, codes, scales, slot, loss_out, grad_out,
    s_row, s_col, t_raw, t_col, t_row, places, slots, differ, got, total,
    loss_z, loss_put, loss_got, loss_sum, send, recv,
):
    r = student.shape[0]
    ds = student.shape[1]
    dt = codes.shape[1]
    group = dt // scales.shape[1]
    a = lax.axis_index("row")
    c = lax.axis_index("col")
    chips = cols_n // 2
    bits = []
    bit = cols_n // 2
    while bit > 1:
        bits.append(bit)
        bit //= 2
    orders = (tuple(bits), tuple(reversed(bits)))
    core = c % 2
    chip = c // 2
    counter = [0]

    def take(count=1):
        counter[0] += count
        return counter[0] - count

    def copy_to(src, dst, index, device):
        return pltpu.make_async_remote_copy(
            src_ref=src, dst_ref=dst, send_sem=send.at[index], recv_sem=recv.at[index],
            device_id=device, device_id_type=MESH,
        )

    def block(index, size=r):
        return pl.ds(pl.multiple_of(index * size, size), size)

    barrier = pltpu.get_barrier_semaphore()
    for k in range(1, rows_n):
        pl.semaphore_signal(barrier, inc=1, device_id=((a + k) % rows_n, c), device_id_type=MESH)
    for bit in bits + [1]:
        pl.semaphore_signal(barrier, inc=1, device_id=(a, flip(c, bit)), device_id_type=MESH)

    slots[a] = jnp.broadcast_to(slot[...], slots.shape[1:])
    cut_rows = r // 2

    def teacher(part):
        rows = slice(part * cut_rows, (part + 1) * cut_rows)
        squares = jnp.zeros((cut_rows, group), F32)
        for g in range(dt // group):
            value = codes[rows, g * group:(g + 1) * group].astype(F32) * scales[rows, g:g + 1].astype(F32)
            squares = squares + value * value
        inverse = lax.rsqrt(jnp.sum(squares, axis=1, keepdims=True) + 1e-06)
        to = block(2 * a + part, cut_rows)
        for g in range(dt // group):
            value = codes[rows, g * group:(g + 1) * group].astype(F32) * scales[rows, g:g + 1].astype(F32)
            t_raw[to, g * group:(g + 1) * group] = (value * inverse).astype(BF16)

    def line(refs):
        base = take(len(refs) * 2 * (rows_n - 1))

        def each(step, up, parts, act):
            for n, (ref, view) in enumerate(refs):
                if n in parts:
                    act(ref, view, base + (n * 2 + up) * (rows_n - 1) + step)

        every_part = tuple(range(len(refs)))

        def start(step, parts=every_part):
            for up in (1, 0):
                held = a - step if up else a + step
                ok = (held >= 0) & (a < rows_n - 1) if up else (held < rows_n) & (a > 0)
                to = (a + 1 if up else a - 1, c)

                @pl.when(ok)
                def _():
                    each(step, up, parts, lambda ref, view, index: copy_to(
                        view(ref, held), view(ref, held), index, to).start())

        def wait_recv(step, parts=every_part):
            for up in (1, 0):
                held = a - 1 - step if up else a + 1 + step
                ok = held >= 0 if up else held < rows_n

                @pl.when(ok)
                def _():
                    each(step, up, parts, lambda ref, view, index: copy_to(
                        view(ref, held), view(ref, held), index, (a, c)).wait_recv())

        def wait_send():
            for step in range(rows_n - 1):
                for up in (1, 0):
                    held = a - step if up else a + step
                    ok = (held >= 0) & (a < rows_n - 1) if up else (held < rows_n) & (a > 0)

                    @pl.when(ok)
                    def _():
                        each(step, up, every_part, lambda ref, view, index: copy_to(
                            view(ref, held), view(ref, held), index, (a, c)).wait_send())

        return start, wait_recv, wait_send

    def plane(ref, width):
        half = width // 2
        started = []
        hops, cores = {}, {}

        def hop(h, step, mask):
            view = ref.at[block(flip_all(c, mask)), h * half:(h + 1) * half]
            hops[h, step, mask] = copy_to(view, view, take(), (a, flip(c, orders[h][step])))
            hops[h, step, mask].start()
            started.append(hops[h, step, mask])

        def to_core(h, mask):
            view = ref.at[block(flip_all(c, mask)), h * half:(h + 1) * half]
            cores[h, mask] = copy_to(view, view, take(), (a, flip(c, 1)))
            cores[h, mask].start()
            started.append(cores[h, mask])

        def start():
            for step in range(len(bits)):
                for h in (0, 1):
                    hop(h, step, 0)
            for h in (0, 1):
                to_core(h, 0)

        def pass_on(step):
            for h in (0, 1):
                masks = [0]
                for bit in orders[h][:step]:
                    masks = masks + [mask + bit for mask in masks]
                for mask in masks:
                    hops[h, step, mask].wait_recv()
                    held = mask + orders[h][step]
                    for later in range(step + 1, len(bits)):
                        hop(h, later, held)
                    to_core(h, held)

        def wait_core():
            for copy in cores.values():
                copy.wait_recv()

        def wait_send():
            for copy in started:
                copy.wait_send()

        return start, pass_on, wait_core, wait_send

    whole = lambda ref, held: ref.at[block(held)]
    page = lambda ref, held: ref.at[held]
    first = lambda ref, held: ref.at[block(2 * held, cut_rows)]
    second = lambda ref, held: ref.at[block(2 * held + 1, cut_rows)]
    t_start, t_recv, t_sent = line([(t_raw, first), (t_raw, second), (slots, page)])
    teacher(0)
    pl.semaphore_wait(barrier, rows_n - 1 + len(bits) + 1)
    t_start(0, (0,))
    teacher(1)
    t_start(0, (1, 2))

    values = student[...].astype(F32)
    inverse_norm = lax.rsqrt(jnp.sum(values * values, axis=1, keepdims=True) + 1e-06)
    unit = (values * inverse_norm).astype(BF16)
    s_row[block(c)] = unit
    s_col[block(a)] = unit

    steps = len(bits)
    p_start, p_pass, p_core, p_sent = plane(s_row, ds)
    p_start()
    for step in range(max(steps, rows_n - 1)):
        if step < rows_n - 1:
            for parts in ((0,), (1, 2)):
                t_recv(step, parts)
                if step + 1 < rows_n - 1:
                    t_start(step + 1, parts)
        if step < steps:
            p_pass(step)

    column = rows_n * r
    for b in range(rows_n):
        at = lax.broadcasted_iota(jnp.int32, (column, r), 0)
        places[:, b * r:(b + 1) * r] = (at == slots[b][0:1, :]).astype(F32).astype(BF16)
    piece = 512

    def own(n, carry):
        cut = block(n, piece)
        t_row[block(c), cut] = jnp.dot(
            places[block(a), :], t_raw[:, cut], preferred_element_type=F32).astype(BF16)
        return carry

    lax.fori_loop(0, dt // piece, own, 0)
    q_start, q_pass, q_core, q_sent = plane(t_row, dt)
    q_start()
    t_sent()
    s_start, s_recv, s_sent = line([(s_col, whole)])
    s_start(0)

    def every(n, carry):
        cut = block(n, piece)
        t_col[:, cut] = jnp.dot(places[...], t_raw[:, cut], preferred_element_type=F32).astype(BF16)
        return carry

    lax.fori_loop(0, dt // piece, every, 0)
    for step in range(max(steps, rows_n - 2)):
        if step < rows_n - 2:
            s_recv(step)
            s_start(step + 1)
        if step < steps:
            q_pass(step)
    p_core()
    q_core()
    q_sent()
    contract = (((1,), (1,)), ((), ()))

    def teacher_gram(i, carry):
        pair = block(i, 2 * r)
        differ[pair, :] = lax.dot_general(
            t_row[pair, :], t_col[...], contract, preferred_element_type=F32)
        return carry

    lax.fori_loop(0, chips, teacher_gram, 0)
    s_recv(rows_n - 2)

    loss_sum[...] = jnp.zeros_like(loss_sum)
    half = ds // 2
    core_base = take(chips)
    away_base = take(2 * chips)
    back = tuple(tuple(reversed(order)) for order in orders)

    def moved(index, mask):
        bit = 1
        while bit < chips:
            index = index + ((mask // bit) % 2) * bit * (1 - 2 * ((index // bit) % 2))
            bit *= 2
        return index

    def core_copy(turn):
        there = moved(chip, turn)
        return copy_to(
            t_row.at[block(there * 2 + 1 - core), 0:ds], t_raw.at[block(turn), 0:ds], core_base + turn, (a, flip(c, 1)))

    def away_copy(h, turn, bit):
        there = moved(chip, turn) * 2 + core
        return copy_to(
            t_row.at[block(there), h * half:(h + 1) * half], got.at[h * chips + turn],
            away_base + h * chips + turn, (a, flip(c, bit)))

    def tile(i, carry):
        turn = chips - 1 - i
        pair = block(moved(chip, turn), 2 * r)
        now = lax.dot_general(s_row[pair, :], s_col[...], contract, preferred_element_type=F32) - differ[pair, :]
        loss_sum[...] += jnp.sum(now * now, axis=0, keepdims=True)
        low = now.astype(BF16)
        for n in range(ds // piece):
            t_row[pair, n * piece:(n + 1) * piece] = jnp.dot(
                low, s_col[:, n * piece:(n + 1) * piece], preferred_element_type=F32).astype(BF16)
        core_copy(turn).start()

        @pl.when(i > 0)
        def _():
            last = turn + 1
            core_copy(last).wait_recv()
            mine = block(moved(chip, last) * 2 + core)
            t_row[mine, 0:ds] = (
                t_row[mine, 0:ds].astype(F32) + t_raw[block(last), 0:ds].astype(F32)).astype(BF16)
            for h in (0, 1):
                bit = back[h][0]

                @pl.when((last // (bit // 2)) % 2 == 1)
                def _():
                    away_copy(h, last, bit).start()

        return carry

    lax.fori_loop(0, chips, tile, 0)

    loss_z[a] = jnp.broadcast_to(jnp.sum(loss_sum[...], axis=1, keepdims=True), loss_z.shape[1:])
    loss_copies = []
    for k in range(1, rows_n):
        copy = copy_to(loss_z.at[a], loss_z.at[a], take(), ((a + k) % rows_n, c))
        copy.start()
        loss_copies.append(copy)

    core_copy(0).wait_recv()
    total[...] = t_row[block(c), 0:ds].astype(F32) + t_raw[block(0), 0:ds].astype(F32)
    left = [list(range(chips)) for _ in (0, 1)]
    away = []
    for step in range(steps):
        for h in (0, 1):
            bit = back[h][step]
            left[h] = [turn for turn in left[h] if not turn & (bit // 2)]
            for turn in left[h]:
                copy = away_copy(h, turn + bit // 2, bit)
                away.append(copy)
                copy.wait_recv()
                span = slice(h * half, (h + 1) * half)
                landed = got[h * chips + turn + bit // 2].astype(F32)
                if turn == 0:
                    total[:, span] += landed
                else:
                    mine = block(flip_all(c, 2 * turn))
                    t_row[mine, span] = (t_row[mine, span].astype(F32) + landed).astype(BF16)
                    if step + 1 < steps and turn & (back[h][step + 1] // 2):
                        away_copy(h, turn, back[h][step + 1]).start()

    for copy in loss_copies:
        copy.wait_recv()
    loss_now = loss_z[0]
    for b in range(1, rows_n):
        loss_now = loss_now + loss_z[b]
    sent = []
    for step in range(steps):
        loss_put[step] = loss_now
        copy = copy_to(loss_put.at[step], loss_got.at[step], take(), (a, flip(c, bits[step])))
        copy.start()
        copy.wait_recv()
        loss_now = loss_now + loss_got[step]
        sent.append(copy)
    loss_put[steps] = loss_now
    copy = copy_to(loss_put.at[steps], loss_got.at[steps], take(), (a, flip(c, 1)))
    copy.start()
    sent.append(copy)

    grad = total[...] * float(ds)
    values = student[...].astype(F32)
    inverse_norm = lax.rsqrt(jnp.sum(values * values, axis=1, keepdims=True) + 1e-06)
    unit = values * inverse_norm
    along = jnp.sum(unit * grad, axis=1, keepdims=True)
    grad_out[...] = inverse_norm * (grad - unit * along)

    copy.wait_recv()
    loss_out[...] = (loss_now + loss_got[steps]) * (ds / (total_rows * total_rows))

    for copy in sent + loss_copies + away:
        copy.wait_send()
    for i in range(chips):
        core_copy(i).wait_send()
    s_sent()
    p_sent()


def on_device(rows_n, cols_n, student, codes, scales, slot):
    r, ds = student.shape
    dt = codes.shape[1]
    total_rows = r * rows_n * cols_n
    chips = cols_n // 2
    steps = chips.bit_length() - 1
    count = 8 * (rows_n - 1) + 2 * (2 * (chips - 1) + 2 * chips)
    count += chips + 2 * chips + (rows_n - 1) + steps + 1
    vmem = pl.BlockSpec(memory_space=pltpu.VMEM)
    loss, grad = pl.pallas_call(
        functools.partial(kernel, rows_n, cols_n, total_rows),
        out_shape=(jax.ShapeDtypeStruct((8, 128), F32), jax.ShapeDtypeStruct((r, ds), F32)),
        in_specs=[vmem] * 4,
        out_specs=(vmem, vmem),
        scratch_shapes=[
            pltpu.VMEM((cols_n * r, ds), BF16),
            pltpu.VMEM((rows_n * r, ds), BF16),
            pltpu.VMEM((rows_n * r, dt), BF16),
            pltpu.VMEM((rows_n * r, dt), BF16),
            pltpu.VMEM((cols_n * r, dt), BF16),
            pltpu.VMEM((rows_n * r, rows_n * r), BF16),
            pltpu.VMEM((rows_n, 8, r), jnp.int32),
            pltpu.VMEM((cols_n * r, rows_n * r), F32),
            pltpu.VMEM((2 * chips, r, ds // 2), BF16),
            pltpu.VMEM((r, ds), F32),
            pltpu.VMEM((rows_n, 8, 128), F32),
            pltpu.VMEM((steps + 1, 8, 128), F32),
            pltpu.VMEM((steps + 1, 8, 128), F32),
            pltpu.VMEM((1, rows_n * r), F32),
            pltpu.SemaphoreType.DMA((count,)),
            pltpu.SemaphoreType.DMA((count,)),
        ],
        compiler_params=pltpu.CompilerParams(
            collective_id=0, has_side_effects=True, vmem_limit_bytes=62 * 1024 * 1024
        ),
    )(student, codes, scales, slot.reshape(1, r))
    return loss[0, 0], grad


def solution(mesh):
    rows_n, cols_n = mesh.shape["row"], mesh.shape["col"]
    return jax.shard_map(
        functools.partial(on_device, rows_n, cols_n),
        mesh=mesh,
        in_specs=(
            P(("row", "col"), None),
            P(("row", "col"), None),
            P(("row", "col"), None),
            P(("row", "col")),
        ),
        out_specs=(P(), P(("row", "col"), None)),
        check_vma=False,
    )
```

```python
import functools

import jax
import jax.numpy as jnp
from jax import lax
from jax.experimental import pallas as pl
from jax.experimental.pallas import tpu as pltpu
from jax.sharding import PartitionSpec as P

MESH = pl.DeviceIdType.MESH
F32 = jnp.float32
BF16 = jnp.bfloat16


def flip(index, bit):
    return index + bit * (1 - 2 * ((index // bit) % 2))


def flip_all(index, mask):
    bit = 1
    while bit <= mask:
        if mask & bit:
            index = flip(index, bit)
        bit *= 2
    return index


def kernel(
    rows_n, cols_n, total_rows, student, codes, scales, slot, loss_out, grad_out,
    s_row, s_col, t_raw, t_col, t_row, places, slots, differ, got, total,
    loss_z, loss_put, loss_got, loss_sum, send, recv,
):
    r = student.shape[0]
    ds = student.shape[1]
    dt = codes.shape[1]
    group = dt // scales.shape[1]
    a = lax.axis_index("row")
    c = lax.axis_index("col")
    chips = cols_n // 2
    bits = []
    bit = cols_n // 2
    while bit > 1:
        bits.append(bit)
        bit //= 2
    orders = (tuple(bits), tuple(reversed(bits)))
    core = c % 2
    chip = c // 2
    counter = [0]

    def take(count=1):
        counter[0] += count
        return counter[0] - count

    def copy_to(src, dst, index, device):
        return pltpu.make_async_remote_copy(
            src_ref=src, dst_ref=dst, send_sem=send.at[index], recv_sem=recv.at[index],
            device_id=device, device_id_type=MESH,
        )

    def block(index, size=r):
        return pl.ds(pl.multiple_of(index * size, size), size)

    barrier = pltpu.get_barrier_semaphore()
    for k in range(1, rows_n):
        pl.semaphore_signal(barrier, inc=1, device_id=((a + k) % rows_n, c), device_id_type=MESH)
    for bit in bits + [1]:
        pl.semaphore_signal(barrier, inc=1, device_id=(a, flip(c, bit)), device_id_type=MESH)

    slots[a] = jnp.broadcast_to(slot[...], slots.shape[1:])
    cut_rows = r // 2

    def teacher(part):
        rows = slice(part * cut_rows, (part + 1) * cut_rows)
        squares = jnp.zeros((cut_rows, group), F32)
        for g in range(dt // group):
            value = codes[rows, g * group:(g + 1) * group].astype(F32) * scales[rows, g:g + 1].astype(F32)
            squares = squares + value * value
        inverse = lax.rsqrt(jnp.sum(squares, axis=1, keepdims=True) + 1e-06)
        to = block(2 * a + part, cut_rows)
        for g in range(dt // group):
            value = codes[rows, g * group:(g + 1) * group].astype(F32) * scales[rows, g:g + 1].astype(F32)
            t_raw[to, g * group:(g + 1) * group] = (value * inverse).astype(BF16)

    def line(refs):
        base = take(len(refs) * 2 * (rows_n - 1))

        def each(step, up, parts, act):
            for n, (ref, view) in enumerate(refs):
                if n in parts:
                    act(ref, view, base + (n * 2 + up) * (rows_n - 1) + step)

        every_part = tuple(range(len(refs)))

        def start(step, parts=every_part):
            for up in (1, 0):
                held = a - step if up else a + step
                ok = (held >= 0) & (a < rows_n - 1) if up else (held < rows_n) & (a > 0)
                to = (a + 1 if up else a - 1, c)

                @pl.when(ok)
                def _():
                    each(step, up, parts, lambda ref, view, index: copy_to(
                        view(ref, held), view(ref, held), index, to).start())

        def wait_recv(step, parts=every_part):
            for up in (1, 0):
                held = a - 1 - step if up else a + 1 + step
                ok = held >= 0 if up else held < rows_n

                @pl.when(ok)
                def _():
                    each(step, up, parts, lambda ref, view, index: copy_to(
                        view(ref, held), view(ref, held), index, (a, c)).wait_recv())

        def wait_send():
            for step in range(rows_n - 1):
                for up in (1, 0):
                    held = a - step if up else a + step
                    ok = (held >= 0) & (a < rows_n - 1) if up else (held < rows_n) & (a > 0)

                    @pl.when(ok)
                    def _():
                        each(step, up, every_part, lambda ref, view, index: copy_to(
                            view(ref, held), view(ref, held), index, (a, c)).wait_send())

        return start, wait_recv, wait_send

    def plane(ref, base, width):
        half = width // 2
        started = []
        hops, cores = {}, {}

        def hop(h, step, mask):
            view = ref.at[block(flip_all(c, mask)), base + h * half:base + (h + 1) * half]
            hops[h, step, mask] = copy_to(view, view, take(), (a, flip(c, orders[h][step])))
            hops[h, step, mask].start()
            started.append(hops[h, step, mask])

        def to_core(h, mask):
            view = ref.at[block(flip_all(c, mask)), base + h * half:base + (h + 1) * half]
            cores[h, mask] = copy_to(view, view, take(), (a, flip(c, 1)))
            cores[h, mask].start()
            started.append(cores[h, mask])

        def start():
            for step in range(len(bits)):
                for h in (0, 1):
                    hop(h, step, 0)
            for h in (0, 1):
                to_core(h, 0)

        def pass_on(step):
            for h in (0, 1):
                masks = [0]
                for bit in orders[h][:step]:
                    masks = masks + [mask + bit for mask in masks]
                for mask in masks:
                    hops[h, step, mask].wait_recv()
                    held = mask + orders[h][step]
                    for later in range(step + 1, len(bits)):
                        hop(h, later, held)
                    to_core(h, held)

        def wait_core():
            for copy in cores.values():
                copy.wait_recv()

        def wait_send():
            for copy in started:
                copy.wait_send()

        return start, pass_on, wait_core, wait_send

    whole = lambda ref, held: ref.at[block(held)]
    page = lambda ref, held: ref.at[held]
    wide = dt // 2
    first = lambda ref, held: ref.at[block(2 * held, cut_rows), 0:wide]
    second = lambda ref, held: ref.at[block(2 * held + 1, cut_rows), 0:wide]
    third = lambda ref, held: ref.at[block(held), wide:dt]
    t_start, t_recv, t_sent = line([(slots, page), (t_raw, first), (t_raw, second), (t_raw, third)])
    teacher(0)
    pl.semaphore_wait(barrier, rows_n - 1 + len(bits) + 1)
    t_start(0, (0, 1))
    teacher(1)
    t_start(0, (2,))

    values = student[...].astype(F32)
    inverse_norm = lax.rsqrt(jnp.sum(values * values, axis=1, keepdims=True) + 1e-06)
    unit = (values * inverse_norm).astype(BF16)
    s_row[block(c)] = unit
    s_col[block(a)] = unit

    steps = len(bits)
    p_start, p_pass, p_core, p_sent = plane(s_row, 0, ds)
    p_start()
    for step in range(max(steps, rows_n - 1)):
        if step < rows_n - 1:
            for parts in ((0, 1), (2,)):
                t_recv(step, parts)
                if step + 1 < rows_n - 1:
                    t_start(step + 1, parts)
        if step < steps:
            p_pass(step)

    t_start(0, (3,))

    column = rows_n * r
    for b in range(rows_n):
        at = lax.broadcasted_iota(jnp.int32, (column, r), 0)
        places[:, b * r:(b + 1) * r] = (at == slots[b][0:1, :]).astype(F32).astype(BF16)
    piece = 512
    narrow = 256
    contract = (((1,), (1,)), ((), ()))

    def own(n, carry):
        cut = block(n, narrow)
        t_row[block(c), cut] = jnp.dot(
            places[block(a), :], t_raw[:, cut], preferred_element_type=F32).astype(BF16)
        return carry

    def every(n, carry):
        cut = block(n, narrow)
        t_col[:, cut] = jnp.dot(places[...], t_raw[:, cut], preferred_element_type=F32).astype(BF16)
        return carry

    def teacher_gram(part):
        def body(i, carry):
            pair = block(i, 2 * r)
            span = slice(part * wide, (part + 1) * wide)
            gram = lax.dot_general(t_row[pair, span], t_col[:, span], contract, preferred_element_type=F32)
            differ[pair, :] = differ[pair, :] + gram if part else gram
            return carry

        lax.fori_loop(0, chips, body, 0)

    count = wide // narrow
    lax.fori_loop(0, count, own, 0)
    q_start, q_pass, q_core, q_sent = plane(t_row, 0, wide)
    q_start()
    lax.fori_loop(0, count, every, 0)
    for step in range(max(steps, rows_n - 2)):
        if step < rows_n - 2:
            t_recv(step, (3,))
            t_start(step + 1, (3,))
        if step < steps:
            q_pass(step)
    q_core()
    teacher_gram(0)
    t_recv(rows_n - 2, (3,))

    lax.fori_loop(count, 2 * count, own, 0)
    u_start, u_pass, u_core, u_sent = plane(t_row, wide, wide)
    u_start()
    t_sent()
    s_start, s_recv, s_sent = line([(s_col, whole)])
    s_start(0)
    lax.fori_loop(count, 2 * count, every, 0)
    for step in range(max(steps, rows_n - 2)):
        if step < rows_n - 2:
            s_recv(step)
            s_start(step + 1)
        if step < steps:
            u_pass(step)
    p_core()
    u_core()
    teacher_gram(1)
    q_sent()
    u_sent()
    s_recv(rows_n - 2)

    loss_sum[...] = jnp.zeros_like(loss_sum)
    half = ds // 2
    core_base = take(chips)
    away_base = take(2 * chips)
    back = tuple(tuple(reversed(order)) for order in orders)

    def moved(index, mask):
        bit = 1
        while bit < chips:
            index = index + ((mask // bit) % 2) * bit * (1 - 2 * ((index // bit) % 2))
            bit *= 2
        return index

    def core_copy(turn):
        there = moved(chip, turn)
        return copy_to(
            t_row.at[block(there * 2 + 1 - core), 0:ds], t_raw.at[block(turn), 0:ds], core_base + turn, (a, flip(c, 1)))

    def away_copy(h, turn, bit):
        there = moved(chip, turn) * 2 + core
        return copy_to(
            t_row.at[block(there), h * half:(h + 1) * half], got.at[h * chips + turn],
            away_base + h * chips + turn, (a, flip(c, bit)))

    def tile(i, carry):
        turn = chips - 1 - i
        pair = block(moved(chip, turn), 2 * r)
        now = lax.dot_general(s_row[pair, :], s_col[...], contract, preferred_element_type=F32) - differ[pair, :]
        loss_sum[...] += jnp.sum(now * now, axis=0, keepdims=True)
        low = now.astype(BF16)
        for n in range(ds // piece):
            t_row[pair, n * piece:(n + 1) * piece] = jnp.dot(
                low, s_col[:, n * piece:(n + 1) * piece], preferred_element_type=F32).astype(BF16)
        core_copy(turn).start()

        @pl.when(i > 0)
        def _():
            last = turn + 1
            core_copy(last).wait_recv()
            mine = block(moved(chip, last) * 2 + core)
            t_row[mine, 0:ds] = (
                t_row[mine, 0:ds].astype(F32) + t_raw[block(last), 0:ds].astype(F32)).astype(BF16)
            for h in (0, 1):
                bit = back[h][0]

                @pl.when((last // (bit // 2)) % 2 == 1)
                def _():
                    away_copy(h, last, bit).start()

        return carry

    lax.fori_loop(0, chips, tile, 0)

    loss_z[a] = jnp.broadcast_to(jnp.sum(loss_sum[...], axis=1, keepdims=True), loss_z.shape[1:])
    loss_copies = []
    for k in range(1, rows_n):
        copy = copy_to(loss_z.at[a], loss_z.at[a], take(), ((a + k) % rows_n, c))
        copy.start()
        loss_copies.append(copy)

    core_copy(0).wait_recv()
    total[...] = t_row[block(c), 0:ds].astype(F32) + t_raw[block(0), 0:ds].astype(F32)
    for copy in loss_copies:
        copy.wait_recv()
    loss_now = loss_z[0]
    for b in range(1, rows_n):
        loss_now = loss_now + loss_z[b]
    sent = []
    left = [list(range(chips)) for _ in (0, 1)]
    away = []
    for step in range(steps):
        loss_put[step] = loss_now
        hop = copy_to(loss_put.at[step], loss_got.at[step], take(), (a, flip(c, bits[step])))
        hop.start()
        sent.append(hop)
        for h in (0, 1):
            bit = back[h][step]
            left[h] = [turn for turn in left[h] if not turn & (bit // 2)]
            for turn in left[h]:
                copy = away_copy(h, turn + bit // 2, bit)
                away.append(copy)
                copy.wait_recv()
                span = slice(h * half, (h + 1) * half)
                landed = got[h * chips + turn + bit // 2].astype(F32)
                if turn == 0:
                    total[:, span] += landed
                else:
                    mine = block(flip_all(c, 2 * turn))
                    t_row[mine, span] = (t_row[mine, span].astype(F32) + landed).astype(BF16)
                    if step + 1 < steps and turn & (back[h][step + 1] // 2):
                        away_copy(h, turn, back[h][step + 1]).start()
        hop.wait_recv()
        loss_now = loss_now + loss_got[step]

    loss_put[steps] = loss_now
    copy = copy_to(loss_put.at[steps], loss_got.at[steps], take(), (a, flip(c, 1)))
    copy.start()
    sent.append(copy)

    grad = total[...] * float(ds)
    values = student[...].astype(F32)
    inverse_norm = lax.rsqrt(jnp.sum(values * values, axis=1, keepdims=True) + 1e-06)
    unit = values * inverse_norm
    along = jnp.sum(unit * grad, axis=1, keepdims=True)
    grad_out[...] = inverse_norm * (grad - unit * along)

    copy.wait_recv()
    loss_out[...] = (loss_now + loss_got[steps]) * (ds / (total_rows * total_rows))

    for copy in sent + loss_copies + away:
        copy.wait_send()
    for i in range(chips):
        core_copy(i).wait_send()
    s_sent()
    p_sent()


def on_device(rows_n, cols_n, student, codes, scales, slot):
    r, ds = student.shape
    dt = codes.shape[1]
    total_rows = r * rows_n * cols_n
    chips = cols_n // 2
    steps = chips.bit_length() - 1
    count = 10 * (rows_n - 1) + 3 * (2 * (chips - 1) + 2 * chips)
    count += chips + 2 * chips + (rows_n - 1) + steps + 1
    vmem = pl.BlockSpec(memory_space=pltpu.VMEM)
    loss, grad = pl.pallas_call(
        functools.partial(kernel, rows_n, cols_n, total_rows),
        out_shape=(jax.ShapeDtypeStruct((8, 128), F32), jax.ShapeDtypeStruct((r, ds), F32)),
        in_specs=[vmem] * 4,
        out_specs=(vmem, vmem),
        scratch_shapes=[
            pltpu.VMEM((cols_n * r, ds), BF16),
            pltpu.VMEM((rows_n * r, ds), BF16),
            pltpu.VMEM((rows_n * r, dt), BF16),
            pltpu.VMEM((rows_n * r, dt), BF16),
            pltpu.VMEM((cols_n * r, dt), BF16),
            pltpu.VMEM((rows_n * r, rows_n * r), BF16),
            pltpu.VMEM((rows_n, 8, r), jnp.int32),
            pltpu.VMEM((cols_n * r, rows_n * r), F32),
            pltpu.VMEM((2 * chips, r, ds // 2), BF16),
            pltpu.VMEM((r, ds), F32),
            pltpu.VMEM((rows_n, 8, 128), F32),
            pltpu.VMEM((steps + 1, 8, 128), F32),
            pltpu.VMEM((steps + 1, 8, 128), F32),
            pltpu.VMEM((1, rows_n * r), F32),
            pltpu.SemaphoreType.DMA((count,)),
            pltpu.SemaphoreType.DMA((count,)),
        ],
        compiler_params=pltpu.CompilerParams(
            collective_id=0, has_side_effects=True, vmem_limit_bytes=62 * 1024 * 1024
        ),
    )(student, codes, scales, slot.reshape(1, r))
    return loss[0, 0], grad


def solution(mesh):
    rows_n, cols_n = mesh.shape["row"], mesh.shape["col"]
    return jax.shard_map(
        functools.partial(on_device, rows_n, cols_n),
        mesh=mesh,
        in_specs=(
            P(("row", "col"), None),
            P(("row", "col"), None),
            P(("row", "col"), None),
            P(("row", "col")),
        ),
        out_specs=(P(), P(("row", "col"), None)),
        check_vma=False,
    )
```

```python
import functools

import jax
import jax.numpy as jnp
from jax import lax
from jax.experimental import pallas as pl
from jax.experimental.pallas import tpu as pltpu
from jax.sharding import PartitionSpec as P

MESH = pl.DeviceIdType.MESH
F32 = jnp.float32
BF16 = jnp.bfloat16


def flip(index, bit):
    return index + bit * (1 - 2 * ((index // bit) % 2))


def flip_all(index, mask):
    bit = 1
    while bit <= mask:
        if mask & bit:
            index = flip(index, bit)
        bit *= 2
    return index


def kernel(
    rows_n, cols_n, total_rows, student, codes, scales, slot, loss_out, grad_out,
    s_row, s_col, t_raw, t_col, t_row, places, slots, differ, got, total,
    loss_z, loss_put, loss_got, loss_sum, send, recv,
):
    r = student.shape[0]
    ds = student.shape[1]
    dt = codes.shape[1]
    group = dt // scales.shape[1]
    a = lax.axis_index("row")
    c = lax.axis_index("col")
    chips = cols_n // 2
    bits = []
    bit = cols_n // 2
    while bit > 1:
        bits.append(bit)
        bit //= 2
    orders = (tuple(bits), tuple(reversed(bits)))
    core = c % 2
    chip = c // 2
    counter = [0]

    def take(count=1):
        counter[0] += count
        return counter[0] - count

    def copy_to(src, dst, index, device):
        return pltpu.make_async_remote_copy(
            src_ref=src, dst_ref=dst, send_sem=send.at[index], recv_sem=recv.at[index],
            device_id=device, device_id_type=MESH,
        )

    def block(index, size=r):
        return pl.ds(pl.multiple_of(index * size, size), size)

    barrier = pltpu.get_barrier_semaphore()
    for k in range(1, rows_n):
        pl.semaphore_signal(barrier, inc=1, device_id=((a + k) % rows_n, c), device_id_type=MESH)
    for bit in bits + [1]:
        pl.semaphore_signal(barrier, inc=1, device_id=(a, flip(c, bit)), device_id_type=MESH)

    slots[a] = jnp.broadcast_to(slot[...], slots.shape[1:])
    cut_rows = r // 2

    def teacher(part):
        rows = slice(part * cut_rows, (part + 1) * cut_rows)
        squares = jnp.zeros((cut_rows, group), F32)
        for g in range(dt // group):
            value = codes[rows, g * group:(g + 1) * group].astype(F32) * scales[rows, g:g + 1].astype(F32)
            squares = squares + value * value
        inverse = lax.rsqrt(jnp.sum(squares, axis=1, keepdims=True) + 1e-06)
        to = block(2 * a + part, cut_rows)
        for g in range(dt // group):
            value = codes[rows, g * group:(g + 1) * group].astype(F32) * scales[rows, g:g + 1].astype(F32)
            t_raw[to, g * group:(g + 1) * group] = (value * inverse).astype(BF16)

    def line(refs):
        base = take(len(refs) * 2 * (rows_n - 1))

        def each(step, up, parts, act):
            for n, (ref, view) in enumerate(refs):
                if n in parts:
                    act(ref, view, base + (n * 2 + up) * (rows_n - 1) + step)

        every_part = tuple(range(len(refs)))

        def start(step, parts=every_part):
            for up in (1, 0):
                held = a - step if up else a + step
                ok = (held >= 0) & (a < rows_n - 1) if up else (held < rows_n) & (a > 0)
                to = (a + 1 if up else a - 1, c)

                @pl.when(ok)
                def _():
                    each(step, up, parts, lambda ref, view, index: copy_to(
                        view(ref, held), view(ref, held), index, to).start())

        def wait_recv(step, parts=every_part):
            for up in (1, 0):
                held = a - 1 - step if up else a + 1 + step
                ok = held >= 0 if up else held < rows_n

                @pl.when(ok)
                def _():
                    each(step, up, parts, lambda ref, view, index: copy_to(
                        view(ref, held), view(ref, held), index, (a, c)).wait_recv())

        def wait_send():
            for step in range(rows_n - 1):
                for up in (1, 0):
                    held = a - step if up else a + step
                    ok = (held >= 0) & (a < rows_n - 1) if up else (held < rows_n) & (a > 0)

                    @pl.when(ok)
                    def _():
                        each(step, up, every_part, lambda ref, view, index: copy_to(
                            view(ref, held), view(ref, held), index, (a, c)).wait_send())

        return start, wait_recv, wait_send

    def plane(ref, base, width):
        half = width // 2
        started = []
        hops, cores = {}, {}

        def hop(h, step, mask):
            view = ref.at[block(flip_all(c, mask)), base + h * half:base + (h + 1) * half]
            hops[h, step, mask] = copy_to(view, view, take(), (a, flip(c, orders[h][step])))
            hops[h, step, mask].start()
            started.append(hops[h, step, mask])

        def to_core(h, mask):
            view = ref.at[block(flip_all(c, mask)), base + h * half:base + (h + 1) * half]
            cores[h, mask] = copy_to(view, view, take(), (a, flip(c, 1)))
            cores[h, mask].start()
            started.append(cores[h, mask])

        def start():
            for step in range(len(bits)):
                for h in (0, 1):
                    hop(h, step, 0)
            for h in (0, 1):
                to_core(h, 0)

        def pass_on(step):
            for h in (0, 1):
                masks = [0]
                for bit in orders[h][:step]:
                    masks = masks + [mask + bit for mask in masks]
                for mask in masks:
                    hops[h, step, mask].wait_recv()
                    held = mask + orders[h][step]
                    for later in range(step + 1, len(bits)):
                        hop(h, later, held)
                    to_core(h, held)

        def wait_core():
            for copy in cores.values():
                copy.wait_recv()

        def wait_send():
            for copy in started:
                copy.wait_send()

        return start, pass_on, wait_core, wait_send

    page = lambda ref, held: ref.at[held]
    wide = dt // 2
    first = lambda ref, held: ref.at[block(2 * held, cut_rows), 0:wide]
    second = lambda ref, held: ref.at[block(2 * held + 1, cut_rows), 0:wide]
    third = lambda ref, held: ref.at[block(2 * held, cut_rows), wide:dt]
    fourth = lambda ref, held: ref.at[block(2 * held + 1, cut_rows), wide:dt]
    upper = lambda ref, held: ref.at[block(2 * held, cut_rows)]
    lower = lambda ref, held: ref.at[block(2 * held + 1, cut_rows)]
    t_start, t_recv, t_sent = line(
        [(slots, page), (t_raw, first), (t_raw, second), (t_raw, third), (t_raw, fourth)])
    teacher(0)
    pl.semaphore_wait(barrier, rows_n - 1 + len(bits) + 1)
    t_start(0, (0, 1))
    teacher(1)
    t_start(0, (2,))

    values = student[...].astype(F32)
    inverse_norm = lax.rsqrt(jnp.sum(values * values, axis=1, keepdims=True) + 1e-06)
    unit = (values * inverse_norm).astype(BF16)
    s_row[block(c)] = unit
    s_col[block(a)] = unit

    steps = len(bits)
    p_start, p_pass, p_core, p_sent = plane(s_row, 0, ds)
    p_start()
    for step in range(max(steps, rows_n - 1)):
        if step < rows_n - 1:
            for parts in ((0, 1), (2,)):
                t_recv(step, parts)
                if step + 1 < rows_n - 1:
                    t_start(step + 1, parts)
        if step < steps:
            p_pass(step)

    t_start(0, (3, 4))

    column = rows_n * r
    for b in range(rows_n):
        at = lax.broadcasted_iota(jnp.int32, (column, r), 0)
        places[:, b * r:(b + 1) * r] = (at == slots[b][0:1, :]).astype(F32).astype(BF16)
    piece = 512
    narrow = 256
    contract = (((1,), (1,)), ((), ()))

    def own(n, carry):
        cut = block(n, narrow)
        t_row[block(c), cut] = jnp.dot(
            places[block(a), :], t_raw[:, cut], preferred_element_type=F32).astype(BF16)
        return carry

    def every(n, carry):
        cut = block(n, narrow)
        t_col[:, cut] = jnp.dot(places[...], t_raw[:, cut], preferred_element_type=F32).astype(BF16)
        return carry

    def teacher_gram(part):
        def body(i, carry):
            pair = block(i, 2 * r)
            span = slice(part * wide, (part + 1) * wide)
            gram = lax.dot_general(t_row[pair, span], t_col[:, span], contract, preferred_element_type=F32)
            differ[pair, :] = differ[pair, :] + gram if part else gram
            return carry

        lax.fori_loop(0, chips, body, 0)

    count = wide // narrow
    lax.fori_loop(0, count, own, 0)
    q_start, q_pass, q_core, q_sent = plane(t_row, 0, wide)
    q_start()
    lax.fori_loop(0, count, every, 0)
    for step in range(max(steps, rows_n - 2)):
        if step < rows_n - 2:
            for parts in ((3,), (4,)):
                t_recv(step, parts)
                t_start(step + 1, parts)
        if step < steps:
            q_pass(step)
    q_core()
    teacher_gram(0)
    t_recv(rows_n - 2, (3, 4))

    lax.fori_loop(count, 2 * count, own, 0)
    u_start, u_pass, u_core, u_sent = plane(t_row, wide, wide)
    u_start()
    t_sent()
    s_start, s_recv, s_sent = line([(s_col, upper), (s_col, lower)])
    s_start(0)
    lax.fori_loop(count, 2 * count, every, 0)
    for step in range(max(steps, rows_n - 2)):
        if step < rows_n - 2:
            for parts in ((0,), (1,)):
                s_recv(step, parts)
                s_start(step + 1, parts)
        if step < steps:
            u_pass(step)
    p_core()
    u_core()
    teacher_gram(1)
    q_sent()
    u_sent()
    s_recv(rows_n - 2)

    loss_sum[...] = jnp.zeros_like(loss_sum)
    half = ds // 2
    core_base = take(chips)
    away_base = take(2 * chips)
    back = tuple(tuple(reversed(order)) for order in orders)

    def moved(index, mask):
        bit = 1
        while bit < chips:
            index = index + ((mask // bit) % 2) * bit * (1 - 2 * ((index // bit) % 2))
            bit *= 2
        return index

    def core_copy(turn):
        there = moved(chip, turn)
        return copy_to(
            t_row.at[block(there * 2 + 1 - core), 0:ds], t_raw.at[block(turn), 0:ds], core_base + turn, (a, flip(c, 1)))

    def away_copy(h, turn, bit):
        there = moved(chip, turn) * 2 + core
        return copy_to(
            t_row.at[block(there), h * half:(h + 1) * half], got.at[h * chips + turn],
            away_base + h * chips + turn, (a, flip(c, bit)))

    def tile(i, carry):
        turn = chips - 1 - i
        pair = block(moved(chip, turn), 2 * r)
        now = lax.dot_general(s_row[pair, :], s_col[...], contract, preferred_element_type=F32) - differ[pair, :]
        loss_sum[...] += jnp.sum(now * now, axis=0, keepdims=True)
        low = now.astype(BF16)
        for n in range(ds // piece):
            t_row[pair, n * piece:(n + 1) * piece] = jnp.dot(
                low, s_col[:, n * piece:(n + 1) * piece], preferred_element_type=F32).astype(BF16)
        core_copy(turn).start()

        @pl.when(i > 0)
        def _():
            last = turn + 1
            core_copy(last).wait_recv()
            mine = block(moved(chip, last) * 2 + core)
            t_row[mine, 0:ds] = (
                t_row[mine, 0:ds].astype(F32) + t_raw[block(last), 0:ds].astype(F32)).astype(BF16)
            for h in (0, 1):
                bit = back[h][0]

                @pl.when((last // (bit // 2)) % 2 == 1)
                def _():
                    away_copy(h, last, bit).start()

        return carry

    lax.fori_loop(0, chips, tile, 0)

    loss_z[a] = jnp.broadcast_to(jnp.sum(loss_sum[...], axis=1, keepdims=True), loss_z.shape[1:])
    loss_copies = []
    for k in range(1, rows_n):
        copy = copy_to(loss_z.at[a], loss_z.at[a], take(), ((a + k) % rows_n, c))
        copy.start()
        loss_copies.append(copy)

    core_copy(0).wait_recv()
    total[...] = t_row[block(c), 0:ds].astype(F32) + t_raw[block(0), 0:ds].astype(F32)
    for copy in loss_copies:
        copy.wait_recv()
    loss_now = loss_z[0]
    for b in range(1, rows_n):
        loss_now = loss_now + loss_z[b]
    sent = []
    left = [list(range(chips)) for _ in (0, 1)]
    away = []
    for step in range(steps):
        loss_put[step] = loss_now
        hop = copy_to(loss_put.at[step], loss_got.at[step], take(), (a, flip(c, bits[step])))
        hop.start()
        sent.append(hop)
        for h in (0, 1):
            bit = back[h][step]
            left[h] = [turn for turn in left[h] if not turn & (bit // 2)]
            for turn in left[h]:
                copy = away_copy(h, turn + bit // 2, bit)
                away.append(copy)
                copy.wait_recv()
                span = slice(h * half, (h + 1) * half)
                landed = got[h * chips + turn + bit // 2].astype(F32)
                if turn == 0:
                    total[:, span] += landed
                else:
                    mine = block(flip_all(c, 2 * turn))
                    t_row[mine, span] = (t_row[mine, span].astype(F32) + landed).astype(BF16)
                    if step + 1 < steps and turn & (back[h][step + 1] // 2):
                        away_copy(h, turn, back[h][step + 1]).start()
        hop.wait_recv()
        loss_now = loss_now + loss_got[step]

    loss_put[steps] = loss_now
    copy = copy_to(loss_put.at[steps], loss_got.at[steps], take(), (a, flip(c, 1)))
    copy.start()
    sent.append(copy)

    grad = total[...] * float(ds)
    values = student[...].astype(F32)
    inverse_norm = lax.rsqrt(jnp.sum(values * values, axis=1, keepdims=True) + 1e-06)
    unit = values * inverse_norm
    along = jnp.sum(unit * grad, axis=1, keepdims=True)
    grad_out[...] = inverse_norm * (grad - unit * along)

    copy.wait_recv()
    loss_out[...] = (loss_now + loss_got[steps]) * (ds / (total_rows * total_rows))

    for copy in sent + loss_copies + away:
        copy.wait_send()
    for i in range(chips):
        core_copy(i).wait_send()
    s_sent()
    p_sent()


def on_device(rows_n, cols_n, student, codes, scales, slot):
    r, ds = student.shape
    dt = codes.shape[1]
    total_rows = r * rows_n * cols_n
    chips = cols_n // 2
    steps = chips.bit_length() - 1
    count = 14 * (rows_n - 1) + 3 * (2 * (chips - 1) + 2 * chips)
    count += chips + 2 * chips + (rows_n - 1) + steps + 1
    vmem = pl.BlockSpec(memory_space=pltpu.VMEM)
    loss, grad = pl.pallas_call(
        functools.partial(kernel, rows_n, cols_n, total_rows),
        out_shape=(jax.ShapeDtypeStruct((8, 128), F32), jax.ShapeDtypeStruct((r, ds), F32)),
        in_specs=[vmem] * 4,
        out_specs=(vmem, vmem),
        scratch_shapes=[
            pltpu.VMEM((cols_n * r, ds), BF16),
            pltpu.VMEM((rows_n * r, ds), BF16),
            pltpu.VMEM((rows_n * r, dt), BF16),
            pltpu.VMEM((rows_n * r, dt), BF16),
            pltpu.VMEM((cols_n * r, dt), BF16),
            pltpu.VMEM((rows_n * r, rows_n * r), BF16),
            pltpu.VMEM((rows_n, 8, r), jnp.int32),
            pltpu.VMEM((cols_n * r, rows_n * r), F32),
            pltpu.VMEM((2 * chips, r, ds // 2), BF16),
            pltpu.VMEM((r, ds), F32),
            pltpu.VMEM((rows_n, 8, 128), F32),
            pltpu.VMEM((steps + 1, 8, 128), F32),
            pltpu.VMEM((steps + 1, 8, 128), F32),
            pltpu.VMEM((1, rows_n * r), F32),
            pltpu.SemaphoreType.DMA((count,)),
            pltpu.SemaphoreType.DMA((count,)),
        ],
        compiler_params=pltpu.CompilerParams(
            collective_id=0, has_side_effects=True, vmem_limit_bytes=62 * 1024 * 1024
        ),
    )(student, codes, scales, slot.reshape(1, r))
    return loss[0, 0], grad


def solution(mesh):
    rows_n, cols_n = mesh.shape["row"], mesh.shape["col"]
    return jax.shard_map(
        functools.partial(on_device, rows_n, cols_n),
        mesh=mesh,
        in_specs=(
            P(("row", "col"), None),
            P(("row", "col"), None),
            P(("row", "col"), None),
            P(("row", "col")),
        ),
        out_specs=(P(), P(("row", "col"), None)),
        check_vma=False,
    )
```
